256 devices in a mesh: section: 16 (over z_lo, y), dp: 16 (over x, z_hi, core).
Axes of the slice: x: 4, y: 4, z: 8 (z_hi: 2, z_lo: 4; z = z_hi * 4 + z_lo), core: 2. Of those that a mesh axis runs over, the one named last changes fastest.
Arguments:
- layer_inputs: bfloat16 [16, 2, 64, 4096], P('section'), may hold values from -6 to 6
- top_grad: bfloat16 [2, 64, 4096], replicated, may hold values from -3 to 3
- w_query: bfloat16 [16, 4096, 4096], P('section', None, 'dp'), may hold values from -1 to 1
- w_keyval: bfloat16 [16, 4096, 1024], P('section', None, 'dp'), may hold values from -1 to 1
- w_out: bfloat16 [16, 4096, 4096], P('section', 'dp'), may hold values from -0.02734375 to 0.02734375
- norm_gain: bfloat16 [16, 4096], P('section'), may hold values from 0.25 to 1.75
- new_block: int32 [16], P('section'), may hold values 0 or 1
Outputs:
- grad_stream: bfloat16 [16, 2, 64, 4096], P('section', None, None, 'dp')
- grad_out_proj: float32 [16, 4096, 4096], P('section', 'dp')
The draws below stay inside these ranges and needn't reach their ends.
All inputs are finite; a program needn't handle non-finite values. No bound on the sum of `new_block` on one device may be relied on, other than what follows from the above.
Results may differ from the reference program's by a relative error of at most 0.035.
Values may be sent and summed in bfloat16 or wider, within the bound.
A program may use at most 64 MiB of HBM per device.

```python
import math
import jax
import jax.numpy as jnp
from jax import lax

D = 4096
HEADS = 32
KVH = 4
HEAD_DIM = 128
TOK = 64
MICRO = 2
LAYERS = 16
N_DP = 16


def draw_layer_inputs(key, part):
    own_key = jax.random.fold_in(key, 29)
    noise_key = jax.random.fold_in(own_key, 0)
    shape = (LAYERS, MICRO, TOK, D)
    values = jnp.clip(jax.random.normal(noise_key, shape, jnp.float32), -6.0, 6.0)
    return values.astype(jnp.bfloat16)


def draw_w_query(key, part):
    own_key = jax.random.fold_in(key, 17)
    shape = (LAYERS, D, HEADS * HEAD_DIM)
    values = jnp.clip(jax.random.normal(own_key, shape, jnp.float32), -6.0, 6.0) / math.sqrt(D)
    return values.astype(jnp.bfloat16)


def draw_w_keyval(key, part):
    own_key = jax.random.fold_in(key, 23)
    shape = (LAYERS, D, 2 * KVH * HEAD_DIM)
    values = jnp.clip(jax.random.normal(own_key, shape, jnp.float32), -6.0, 6.0) / math.sqrt(D)
    return values.astype(jnp.bfloat16)


def set_ends(drawn, stream_key, low, high):
    place = [jax.random.randint(jax.random.fold_in(stream_key, axis), (), 0, length) for axis, length in enumerate(drawn.shape)]
    widest = drawn.shape.index(max(drawn.shape))
    beside = place[:widest] + [(place[widest] + 1) % drawn.shape[widest]] + place[widest + 1:]
    return drawn.at[tuple(place)].set(low).at[tuple(beside)].set(high)


def levels(key, extent, cuts, low, largest):
    def one(position, shards_of):
        draws = jax.random.uniform(jax.random.fold_in(jax.random.fold_in(key, 6), position), (shards_of,), jnp.float32, low / len(cuts), largest / len(cuts))
        return jnp.repeat(jnp.exp(draws), extent[position] // shards_of).reshape((-1,) + (1,) * (len(extent) - position - 1))

    factor_of = one(*cuts[0])
    for cut in cuts[1:]:
        factor_of = factor_of * one(*cut)
    return factor_of


def gaussian(key, dims, width, most, cuts=(), held_as=jnp.bfloat16):
    entries = jax.random.normal(key, dims, jnp.float32) * width
    if len(cuts) > 0:
        entries = levels(key, dims, cuts, -0.22, 0.18) * entries
    return jnp.clip(entries, min=-most, max=most).astype(held_as)


def setup_inputs(seed: int = 0) -> dict:
    splits = jax.random.split(jax.random.key(seed), 8)
    return {
        "layer_inputs": draw_layer_inputs(jax.random.fold_in(splits[7], 71), 0),
        "top_grad": gaussian(splits[1], (MICRO, TOK, D), 0.5, 3.0),
        "w_query": draw_w_query(jax.random.fold_in(splits[7], 71), 0),
        "w_keyval": draw_w_keyval(jax.random.fold_in(splits[7], 71), 0),
        "w_out": gaussian(splits[4], (LAYERS, HEADS * HEAD_DIM, D), (0.3 / (HEADS * HEAD_DIM) ** 0.5), 0.02734375, ((0, 16), (1, 16))),
        "norm_gain": jnp.clip(1.0 + 0.15 * jax.random.normal(splits[5], (LAYERS, D), jnp.float32), 0.25, 1.75).astype(jnp.bfloat16),
        "new_block": set_ends((jax.random.randint(splits[6], (LAYERS,), 0, 3) < 1).astype(jnp.int32), jax.random.fold_in(splits[6], 1), 0, 1),
    }


EPS = 1e-05

def layer_backward(inputs, upstream, w_query, w_keyval, w_out, norm_gain):
    tokens = inputs.shape[0]
    group_size = HEADS // KVH
    local_heads = HEADS // N_DP
    scale_factor = HEAD_DIM ** (-0.5)
    inputs_f = inputs.astype(jnp.float32)
    inverse_rms = lax.rsqrt(lax.optimization_barrier(jnp.mean(inputs_f * inputs_f, axis=-1, keepdims=True)) + EPS)
    gain = norm_gain.astype(jnp.float32)
    normed = (inputs_f * inverse_rms * gain).astype(jnp.bfloat16)
    queries = jnp.dot(normed, w_query, preferred_element_type=jnp.float32).astype(jnp.bfloat16)
    queries = queries.reshape(tokens, HEADS, HEAD_DIM).astype(jnp.float32)
    keyval = jnp.dot(normed, w_keyval, preferred_element_type=jnp.float32).astype(jnp.bfloat16)
    keyval = keyval.reshape(tokens, KVH, 2, HEAD_DIM).astype(jnp.float32)
    key_heads = jnp.repeat(keyval[:, :, 0], group_size, axis=1)
    value_heads = jnp.repeat(keyval[:, :, 1], group_size, axis=1)
    scores = jnp.einsum('thd,shd->hts', queries, key_heads) * scale_factor
    causal = jnp.arange(tokens)[:, None] >= jnp.arange(tokens)[None, :]
    scores = jnp.where(causal[None], scores, -1e+30)
    probs = jax.nn.softmax(scores, axis=-1)
    probs_low = lax.optimization_barrier(probs.astype(jnp.bfloat16)).astype(jnp.float32)
    attended = jnp.einsum('hts,shd->thd', probs_low, value_heads).astype(jnp.bfloat16)
    attended_flat = attended.reshape(tokens, HEADS * HEAD_DIM)
    out_grad = jnp.dot(upstream, w_out.T, preferred_element_type=jnp.float32).astype(jnp.bfloat16)
    out_grad = out_grad.reshape(tokens, HEADS, HEAD_DIM).astype(jnp.float32)
    weight_grad = jnp.dot(attended_flat.T, upstream, preferred_element_type=jnp.float32)
    prob_grad = jnp.einsum('thd,shd->hts', out_grad, value_heads)
    row_delta = lax.optimization_barrier(jnp.sum(probs * prob_grad, axis=-1, keepdims=True))
    score_grad = lax.optimization_barrier((probs * (prob_grad - row_delta)).astype(jnp.bfloat16)).astype(jnp.float32)
    query_grad = (jnp.einsum('hts,shd->thd', score_grad, key_heads) * scale_factor).astype(jnp.bfloat16)
    key_grad = jnp.einsum('hts,thd->shd', score_grad, queries) * scale_factor
    value_grad = jnp.einsum('hts,thd->shd', probs_low, out_grad)
    key_dev = lax.optimization_barrier(jnp.sum(key_grad.reshape(tokens, N_DP, local_heads, HEAD_DIM), axis=2))
    value_dev = lax.optimization_barrier(jnp.sum(value_grad.reshape(tokens, N_DP, local_heads, HEAD_DIM), axis=2))
    keyval_dev = jnp.concatenate([key_dev, value_dev], axis=-1).astype(jnp.bfloat16)
    query_dev = query_grad.reshape(tokens, N_DP, local_heads * HEAD_DIM)
    query_cols = w_query.reshape(w_query.shape[0], N_DP, local_heads * HEAD_DIM)
    keyval_cols = w_keyval.reshape(w_keyval.shape[0], KVH, 2 * HEAD_DIM)

    def device_term(index):
        head_pos = index * local_heads // group_size
        query_part = query_dev[:, index]
        query_weight = query_cols[:, index]
        keyval_part = keyval_dev[:, index]
        keyval_weight = keyval_cols[:, head_pos]
        partial_value = jnp.dot(query_part, query_weight.T, preferred_element_type=jnp.float32)
        partial_value = partial_value + jnp.dot(keyval_part, keyval_weight.T, preferred_element_type=jnp.float32)
        return lax.optimization_barrier(partial_value.astype(jnp.bfloat16)).astype(jnp.float32)
    partials = lax.map(device_term, jnp.arange(N_DP).astype(jnp.int32))
    summed = lax.optimization_barrier(jnp.sum(partials, axis=0))
    norm_grad = lax.optimization_barrier(summed.astype(jnp.bfloat16)).astype(jnp.float32)
    scaled = norm_grad * gain
    row_stat = lax.optimization_barrier(jnp.sum(scaled * inputs_f, axis=-1, keepdims=True)) / inputs_f.shape[1]
    result = upstream.astype(jnp.float32) + inverse_rms * scaled - inputs_f * inverse_rms ** 3 * row_stat
    return (result.astype(jnp.bfloat16), weight_grad)

def reference(layer_inputs, top_grad, w_query, w_keyval, w_out, norm_gain, new_block):
    upstream = [top_grad[micro_pos] for micro_pos in range(MICRO)]
    streams = [None] * LAYERS
    grads = [None] * LAYERS
    for layer_pos in reversed(range(LAYERS)):
        results = []
        total = jnp.zeros((HEADS * HEAD_DIM, D), jnp.float32)
        for micro_pos in range(MICRO):
            result, weight_grad = layer_backward(layer_inputs[layer_pos, micro_pos], upstream[micro_pos], w_query[layer_pos], w_keyval[layer_pos], w_out[layer_pos], norm_gain[layer_pos])
            results.append(result)
            total = total + weight_grad
            upstream[micro_pos] = result
        streams[layer_pos] = jnp.stack(results)
        grads[layer_pos] = total * new_block[layer_pos].astype(jnp.float32)
    return (jnp.stack(streams), jnp.stack(grads))
```

```python
import jax
import jax.numpy as jnp
from jax import lax
from jax.experimental import pallas as pl
from jax.experimental.pallas import tpu as pltpu
from jax.sharding import PartitionSpec as P

HEAD_DIM = 128
EPS = 1e-05
MESH = pl.DeviceIdType.MESH
F32 = jnp.float32
BF16 = jnp.bfloat16

SECTIONS = 16
TOKENS = 64
MICRO = 2
WIDTH = 4096
ROWS = 16
PARTS = TOKENS // ROWS
CHUNKS = MICRO * PARTS
LAG = 2
BLOCK = 256
SLICE = 2 * BLOCK
SCALE = HEAD_DIM ** (-0.5)

SLICES = [(2, 1), (2, 0), (1, 1), (1, 0), (3, 1), (3, 0), (0, 1), (0, 0)]
PEERS = [(dx, dz, dc) for dx, dc in SLICES for dz in (1, 0)][:-1]


def dot(a, b, ca=1, cb=0):
    return lax.dot_general(a, b, (((ca,), (cb,)), ((), ())), preferred_element_type=F32)


def columns(block):
    return pl.ds(pl.multiple_of(block * BLOCK, BLOCK), BLOCK)


def slice_blocks(index):
    return [(index // 2) * 4 + half * 2 + index % 2 for half in range(2)]


def kernel(
    x_ref, top_ref, wq_ref, wkv_ref, wo_ref, gain_ref,
    out_ref, grad_ref,
    wc, wot, normed, r_buf, q_hat, q_low, kv_hat, k_low, v_low, p_buf, p_low, att, dkv_acc,
    g_buf, part_buf, rs_buf, ag_buf, grad_buf,
    rs_send, rs_recv, ag_send, ag_recv, kv_send, kv_recv, grad_sem, gate,
):
    s = lax.axis_index("section")
    d = lax.axis_index("dp")
    x_pos = d // 4
    z_pos = d // 2 % 2
    c_pos = d % 2

    def peer(dx, dz, dc):
        return (x_pos + dx) % 4 * 4 + (z_pos + dz) % 2 * 2 + (c_pos + dc) % 2

    barrier = pltpu.get_barrier_semaphore()

    def greet(section, device):
        pl.semaphore_signal(barrier, inc=1, device_id=(section, device), device_id_type=MESH)

    for offset in PEERS:
        greet(s, peer(*offset))

    @pl.when(s > 0)
    def _():
        for dx, dc in SLICES:
            greet(s - 1, peer(dx, 0, dc))

    @pl.when(s < SECTIONS - 1)
    def _():
        for dx, dc in SLICES:
            greet(s + 1, peer(dx, 0, dc))

    @pl.when(s < SECTIONS - 4)
    def _():
        greet(s + 4, d)

    kv_row = pl.multiple_of(BLOCK + (z_pos * 2 + c_pos) * 64, 64)
    for b in range(WIDTH // BLOCK):
        rows = slice(b * BLOCK, (b + 1) * BLOCK)
        wc[pl.ds(kv_row, 64), rows] = wkv_ref[rows, :].T

    greetings = (
        len(PEERS)
        + jnp.where(s > 0, len(SLICES), 0)
        + jnp.where(s < SECTIONS - 1, len(SLICES), 0)
        + jnp.where(s >= 4, 1, 0)
    )
    pl.semaphore_wait(barrier, greetings)

    def kv_copy(row, device, sem):
        part = wc.at[pl.ds(row, 64)]
        return pltpu.make_async_remote_copy(
            src_ref=part, dst_ref=part, send_sem=kv_send.at[sem], recv_sem=kv_recv.at[sem],
            device_id=(s, device), device_id_type=MESH,
        )

    own_near = kv_copy(kv_row, peer(0, 0, 1), 0)
    own_near.start()

    @pl.when(s < SECTIONS - 4)
    def _():
        pl.semaphore_wait(gate, 1)

    own_far = kv_copy(kv_row, peer(0, 1, 0), 1)
    own_far.start()

    for i in range(CHUNKS):
        m, first = i % 2, (PARTS - 1 - i // 2) * ROWS
        xf = x_ref[m, first : first + ROWS, :].astype(F32)
        r = lax.rsqrt(jnp.mean(xf * xf, axis=-1, keepdims=True) + EPS)
        r_buf[i] = r
        normed[i * ROWS : (i + 1) * ROWS, :] = (xf * r * gain_ref[...]).astype(BF16)
    queries = dot(normed[...], wq_ref[...])
    for i in range(CHUNKS):
        rows = slice(i * ROWS, (i + 1) * ROWS)
        for h in range(2):
            part = queries[rows, h * HEAD_DIM : (h + 1) * HEAD_DIM]
            q_hat[i, h * ROWS : (h + 1) * ROWS, :] = part
            q_low[i, h * ROWS : (h + 1) * ROWS, :] = part.astype(BF16)
    for b in range(WIDTH // BLOCK):
        rows = slice(b * BLOCK, (b + 1) * BLOCK)
        wc[:BLOCK, rows] = wq_ref[rows, :].T
    for i in range(8):
        for half, b in enumerate(slice_blocks(i)):
            first = (2 * i + half) * BLOCK
            wot[first : first + BLOCK, :] = wo_ref[:, b * BLOCK : (b + 1) * BLOCK].T
    dkv_acc[...] = jnp.zeros_like(dkv_acc)

    @pl.when(s == SECTIONS - 1)
    def _():
        for k in range(CHUNKS):
            m, first = k % 2, (PARTS - 1 - k // 2) * ROWS
            for i in range(8):
                for half, b in enumerate(slice_blocks(i)):
                    g_buf[k, i, :, half * BLOCK : (half + 1) * BLOCK] = top_ref[
                        m, first : first + ROWS, b * BLOCK : (b + 1) * BLOCK
                    ]

    far_row = pl.multiple_of(BLOCK + ((1 - z_pos) * 2 + c_pos) * 64, 64)
    far_near_row = pl.multiple_of(BLOCK + ((1 - z_pos) * 2 + 1 - c_pos) * 64, 64)
    near_row = pl.multiple_of(BLOCK + (z_pos * 2 + 1 - c_pos) * 64, 64)
    kv_copy(far_row, peer(0, 1, 0), 1).wait_recv()

    @pl.when(s >= 4)
    def _():
        pl.semaphore_signal(gate, inc=1, device_id=(s - 4, d), device_id_type=MESH)

    far_near = kv_copy(far_row, peer(0, 0, 1), 2)
    far_near.start()
    kv_copy(near_row, peer(0, 0, 1), 0).wait_recv()
    kv_copy(far_near_row, peer(0, 0, 1), 2).wait_recv()
    own_near.wait_send()
    own_far.wait_send()
    far_near.wait_send()

    keyval = dot(normed[...], wc[BLOCK:, :], 1, 1)
    for i in range(CHUNKS):
        m, first = i % 2, (PARTS - 1 - i // 2) * ROWS
        part = keyval[i * ROWS : (i + 1) * ROWS, :]
        kv_hat[i] = part
        k_low[m, first : first + ROWS, :] = part[:, :HEAD_DIM].astype(BF16)
        v_low[m, first : first + ROWS, :] = part[:, HEAD_DIM:].astype(BF16)
    for i in range(CHUNKS):
        m, first = i % 2, (PARTS - 1 - i // 2) * ROWS
        scores = dot(q_low[i], k_low[m], 1, 1) * SCALE
        row = lax.rem(lax.broadcasted_iota(jnp.int32, scores.shape, 0), ROWS) + first
        scores = jnp.where(row >= lax.broadcasted_iota(jnp.int32, scores.shape, 1), scores, -1e30)
        scores = jnp.exp(scores - jnp.max(scores, axis=-1, keepdims=True))
        probs = scores / jnp.sum(scores, axis=-1, keepdims=True)
        p_buf[i] = probs
        low = probs.astype(BF16)
        p_low[i] = low
        attended = dot(low, v_low[m]).astype(BF16)
        for h in range(2):
            att[i, :, h * HEAD_DIM : (h + 1) * HEAD_DIM] = attended[h * ROWS : (h + 1) * ROWS, :]

    own_slice = x_pos * 2 + c_pos

    def ag_copy(k, offset):
        return pltpu.make_async_remote_copy(
            src_ref=ag_buf.at[k], dst_ref=g_buf.at[k, own_slice],
            send_sem=ag_send.at[k], recv_sem=ag_recv.at[k],
            device_id=(s - 1, peer(offset[0], 0, offset[1])), device_id_type=MESH,
        )

    def all_of(ref, sem):
        return pltpu.make_async_copy(ref, ref, sem)

    def first_half(k):
        m = k % 2
        first = pl.multiple_of((PARTS - 1 - k // 2) * ROWS, ROWS)

        @pl.when(s < SECTIONS - 1)
        def _():
            all_of(g_buf.at[k], ag_recv.at[k]).wait()

        g = jnp.concatenate([g_buf[k, i] for i in range(8)], axis=1)
        og = dot(g, wot[...]).astype(BF16)
        og = jnp.concatenate([og[:, :HEAD_DIM], og[:, HEAD_DIM:]], axis=0)
        prob_grad = dot(og, v_low[m], 1, 1)
        probs = p_buf[k]
        delta = jnp.sum(probs * prob_grad, axis=-1, keepdims=True)
        score_grad = (probs * (prob_grad - delta)).astype(BF16)
        dq = (dot(score_grad, k_low[m]) * SCALE).astype(BF16)
        dkv_acc[m, :, :HEAD_DIM] += dot(score_grad, q_low[k], 0, 0) * SCALE
        dkv_acc[m, :, HEAD_DIM:] += dot(p_low[k], og, 0, 0)
        dkv = dkv_acc[m, pl.ds(first, ROWS), :].astype(BF16)
        stat = jnp.sum(dq.astype(F32) * q_hat[k], axis=-1, keepdims=True)
        stat = stat[:ROWS] + stat[ROWS:]
        stat += jnp.sum(dkv.astype(F32) * kv_hat[k], axis=-1, keepdims=True)
        r = r_buf[k]
        stat = stat * (r * r / WIDTH)
        grads = jnp.concatenate([dq[:ROWS], dq[ROWS:], dkv], axis=1)
        for j, (dx, dc) in enumerate(SLICES):
            base = (x_pos + dx) % 4 * 4 + (c_pos + dc) % 2
            for half in range(2):
                block = columns(base + half * 2)
                part = dot(grads, wc[:, block])
                xb = x_ref[m, pl.ds(first, ROWS), block].astype(F32)
                part = part * (r * gain_ref[:, block]) - xb * stat
                part_buf[k, j, :, half * BLOCK : (half + 1) * BLOCK] = part.astype(BF16)
            for dz in (1, 0):
                if (dx, dz, dc) == (0, 0, 0):
                    continue
                pltpu.make_async_remote_copy(
                    src_ref=part_buf.at[k, j], dst_ref=rs_buf.at[k, PEERS.index((dx, dz, dc))],
                    send_sem=rs_send.at[k], recv_sem=rs_recv.at[k],
                    device_id=(s, peer(dx, dz, dc)), device_id_type=MESH,
                ).start()

    def second_half(k):
        m = k % 2
        first = pl.multiple_of((PARTS - 1 - k // 2) * ROWS, ROWS)
        total = g_buf[k, own_slice].astype(F32) + part_buf[k, len(SLICES) - 1].astype(F32)
        all_of(rs_buf.at[k], rs_recv.at[k]).wait()
        for j in range(len(PEERS)):
            total += rs_buf[k, j].astype(F32)
        result = total.astype(BF16)
        ag_buf[k] = result

        @pl.when(s > 0)
        def _():
            for offset in SLICES:
                ag_copy(k, offset).start()

        out_ref[m, pl.ds(first, ROWS), :] = jnp.where(
            z_pos == 0, result[:, :BLOCK], result[:, BLOCK:]
        )

    def grad_copy(i):
        part = pl.ds(i * 1024, 1024)
        return pltpu.make_async_copy(grad_buf.at[:, part], grad_ref.at[:, part], grad_sem.at[i])

    def weight_grad():
        attended = att[...].reshape(CHUNKS * ROWS, BLOCK)
        for i in range(8):
            g = g_buf[:, i].reshape(CHUNKS * ROWS, SLICE)
            part = dot(attended, g, 0, 0)
            for half, b in enumerate(slice_blocks(i)):
                grad_buf[:, b * BLOCK : (b + 1) * BLOCK] = part[:, half * BLOCK : (half + 1) * BLOCK]
            if i % 2 == 1:
                grad_copy(i // 2).start()

    grad_step = jnp.where(s == 0, CHUNKS, CHUNKS + LAG)

    def step(k, carry):
        @pl.when(k < CHUNKS)
        def _():
            first_half(k)

        @pl.when(k == grad_step)
        def _():
            weight_grad()

        @pl.when((k >= LAG) & (k < CHUNKS + LAG))
        def _():
            second_half(k - LAG)

        return carry

    lax.fori_loop(0, CHUNKS + LAG + 1, step, 0)

    for i in range(4):
        grad_copy(i).wait()

    def drain(k, carry):
        all_of(rs_buf.at[k], rs_send.at[k]).wait()

        @pl.when(s > 0)
        def _():
            all_of(g_buf.at[k], ag_send.at[k]).wait()

        return carry

    lax.fori_loop(0, CHUNKS, drain, 0)


def relay(x, top, wq, wkv, wo, gain):
    vmem = pl.BlockSpec(memory_space=pltpu.VMEM)
    return pl.pallas_call(
        kernel,
        out_shape=(
            jax.ShapeDtypeStruct((MICRO, TOKENS, BLOCK), BF16),
            jax.ShapeDtypeStruct((BLOCK, WIDTH), F32),
        ),
        in_specs=[vmem] * 6,
        out_specs=(vmem, pl.BlockSpec(memory_space=pl.ANY)),
        scratch_shapes=[
            pltpu.VMEM((2 * BLOCK, WIDTH), BF16),
            pltpu.VMEM((WIDTH, BLOCK), BF16),
            pltpu.VMEM((CHUNKS * ROWS, WIDTH), BF16),
            pltpu.VMEM((CHUNKS, ROWS, 1), F32),
            pltpu.VMEM((CHUNKS, 2 * ROWS, HEAD_DIM), F32),
            pltpu.VMEM((CHUNKS, 2 * ROWS, HEAD_DIM), BF16),
            pltpu.VMEM((CHUNKS, ROWS, BLOCK), F32),
            pltpu.VMEM((MICRO, TOKENS, HEAD_DIM), BF16),
            pltpu.VMEM((MICRO, TOKENS, HEAD_DIM), BF16),
            pltpu.VMEM((CHUNKS, 2 * ROWS, TOKENS), F32),
            pltpu.VMEM((CHUNKS, 2 * ROWS, TOKENS), BF16),
            pltpu.VMEM((CHUNKS, ROWS, BLOCK), BF16),
            pltpu.VMEM((MICRO, TOKENS, BLOCK), F32),
            pltpu.VMEM((CHUNKS, 8, ROWS, SLICE), BF16),
            pltpu.VMEM((CHUNKS, 8, ROWS, SLICE), BF16),
            pltpu.VMEM((CHUNKS, len(PEERS), ROWS, SLICE), BF16),
            pltpu.VMEM((CHUNKS, ROWS, SLICE), BF16),
            pltpu.VMEM((BLOCK, WIDTH), F32),
            pltpu.SemaphoreType.DMA((CHUNKS,)),
            pltpu.SemaphoreType.DMA((CHUNKS,)),
            pltpu.SemaphoreType.DMA((CHUNKS,)),
            pltpu.SemaphoreType.DMA((CHUNKS,)),
            pltpu.SemaphoreType.DMA((3,)),
            pltpu.SemaphoreType.DMA((3,)),
            pltpu.SemaphoreType.DMA((4,)),
            pltpu.SemaphoreType.REGULAR,
        ],
        compiler_params=pltpu.CompilerParams(
            collective_id=0, has_side_effects=True, vmem_limit_bytes=48 * 1024 * 1024
        ),
        name="relay",
    )(x, top, wq, wkv, wo, gain)


def body(layer_inputs, top_grad, w_query, w_keyval, w_out, norm_gain, new_block):
    stream, grad = relay(
        layer_inputs[0], top_grad, w_query[0], w_keyval[0], w_out[0], norm_gain.astype(F32)
    )
    return stream[None], (grad * new_block[0].astype(F32))[None]


def solution(mesh):
    in_specs = (
        P("section", None, None, None),
        P(),
        P("section", None, "dp"),
        P("section", None, "dp"),
        P("section", "dp", None),
        P("section", None),
        P("section"),
    )
    out_specs = (P("section", None, None, "dp"), P("section", "dp", None))
    return jax.shard_map(body, mesh=mesh, in_specs=in_specs, out_specs=out_specs, check_vma=False)
```

```python
import jax
import jax.numpy as jnp
from jax import lax
from jax.experimental import pallas as pl
from jax.experimental.pallas import tpu as pltpu
from jax.sharding import PartitionSpec as P

HEAD_DIM = 128
EPS = 1e-05
MESH = pl.DeviceIdType.MESH
F32 = jnp.float32
BF16 = jnp.bfloat16

SECTIONS = 16
TOKENS = 64
MICRO = 2
WIDTH = 4096
ROWS = 16
PARTS = TOKENS // ROWS
CHUNKS = MICRO * PARTS
LAG = 1
BLOCK = 256
SLICE = 2 * BLOCK
SCALE = HEAD_DIM ** (-0.5)

HOPS = (2, 1, 3, 0)
PEERS = [(dx, dz) for dx in HOPS for dz in (1, 0)][:-1]
PIECES = 4


def dot(a, b, ca=1, cb=0):
    return lax.dot_general(a, b, (((ca,), (cb,)), ((), ())), preferred_element_type=F32)


def columns(block):
    return pl.ds(pl.multiple_of(block * BLOCK, BLOCK), BLOCK)


def slice_blocks(index):
    return [(index // 2) * 4 + half * 2 + index % 2 for half in range(2)]


def place(k):
    return k % 2, (PARTS - 1 - k // 2) * ROWS


def kernel(
    x_hbm, top_hbm, wq_hbm, wkv_hbm, wo_hbm, gain_ref,
    out_ref, att, g_out,
    x_ref, top_ref, wq_ref, wo_ref,
    wc, wot, normed, r_buf, q_hat, q_low, kvt, k_t, v_t, k_low, v_low, p_buf, p_low_t, dkv_acc,
    g_buf, near_out, near_in, part_buf, rs_buf, ag_buf,
    load_sem, near_send, near_recv, rs_send, rs_recv, ag_send, ag_recv,
    kv_send, kv_recv, far_send, far_recv, pass_send, pass_recv, gate,
):
    s = lax.axis_index("section")
    d = lax.axis_index("dp")
    x_pos = d // 4
    z_pos = d // 2 % 2
    c_pos = d % 2
    top_section = s == SECTIONS - 1

    def peer(dx, dz, dc):
        return (x_pos + dx) % 4 * 4 + (z_pos + dz) % 2 * 2 + (c_pos + dc) % 2

    def all_of(ref, sem):
        return pltpu.make_async_copy(ref, ref, sem)

    def remote(src, dst, send, recv, section, device):
        return pltpu.make_async_remote_copy(
            src_ref=src, dst_ref=dst, send_sem=send, recv_sem=recv,
            device_id=(section, device), device_id_type=MESH,
        )

    own_row = pl.multiple_of((z_pos * 2 + c_pos) * 64, 64)
    near_row = pl.multiple_of((z_pos * 2 + 1 - c_pos) * 64, 64)
    far_row = pl.multiple_of(((1 - z_pos) * 2 + c_pos) * 64, 64)
    cross_row = pl.multiple_of(((1 - z_pos) * 2 + 1 - c_pos) * 64, 64)

    def wc_rows(row):
        return wc.at[pl.ds(pl.multiple_of(BLOCK + row, 64), 64)]

    load_x = pltpu.make_async_copy(x_hbm, x_ref, load_sem.at[0])
    load_kv = pltpu.make_async_copy(wkv_hbm, wc_rows(own_row), load_sem.at[1])
    load_q = pltpu.make_async_copy(wq_hbm, wq_ref, load_sem.at[2])
    load_o = pltpu.make_async_copy(wo_hbm, wo_ref, load_sem.at[3])
    load_top = pltpu.make_async_copy(top_hbm, top_ref, load_sem.at[4])
    for load in (load_x, load_kv, load_q, load_o):
        load.start()

    @pl.when(top_section)
    def _():
        load_top.start()

    barrier = pltpu.get_barrier_semaphore()

    def greet(section, device):
        pl.semaphore_signal(barrier, inc=1, device_id=(section, device), device_id_type=MESH)

    for dx, dz in PEERS:
        greet(s, peer(dx, dz, 0))
    greet(s, peer(0, 0, 1))
    greet(s, peer(0, 1, 1))

    @pl.when(s > 0)
    def _():
        for dx in HOPS:
            for dc in range(2):
                greet(s - 1, peer(dx, 0, dc))

    @pl.when(s < SECTIONS - 1)
    def _():
        for dx in HOPS:
            for dc in range(2):
                greet(s + 1, peer(dx, 0, dc))

    @pl.when(s < SECTIONS - 4)
    def _():
        greet(s + 4, d)

    load_x.wait()
    for m in range(MICRO):
        for first in range(0, TOKENS, ROWS):
            xf = x_ref[m, first : first + ROWS, :].astype(F32)
            r = lax.rsqrt(jnp.mean(xf * xf, axis=-1, keepdims=True) + EPS)
            r_buf[m, first : first + ROWS, :] = r
            rows = slice(m * TOKENS + first, m * TOKENS + first + ROWS)
            normed[rows, :] = (xf * r * gain_ref[...].astype(F32)).astype(BF16)
    load_kv.wait()
    kvt[pl.ds(own_row, 64), :] = dot(wc[pl.ds(BLOCK + own_row, 64), :], normed[...], 1, 1).astype(BF16)

    greetings = (
        len(PEERS) + 2
        + jnp.where(s > 0, 8, 0)
        + jnp.where(s < SECTIONS - 1, 8, 0)
        + jnp.where(s >= 4, 1, 0)
    )
    pl.semaphore_wait(barrier, greetings)

    own_kvt = kvt.at[pl.ds(own_row, 64)]
    kvt_copies = [
        remote(own_kvt, own_kvt, kv_send.at[i], kv_recv.at[i], s, peer(0, dz, dc))
        for i, (dz, dc) in enumerate([(1, 0), (1, 1), (0, 1)])
    ]
    for copy in kvt_copies:
        copy.start()

    def piece(row, i):
        width = WIDTH // PIECES
        return wc.at[pl.ds(pl.multiple_of(BLOCK + row, 64), 64), pl.ds(i * width, width)]

    def across(row, i):
        part = piece(row, i)
        return remote(part, part, far_send.at[i], far_recv.at[i], s, peer(0, 1, 0))

    def beside(row, i, sem):
        part = piece(row, i)
        return remote(part, part, pass_send.at[sem], pass_recv.at[sem], s, peer(0, 0, 1))

    @pl.when(s >= SECTIONS - 4)
    def _():
        for i in range(PIECES):
            across(own_row, i).start()

    for i in range(PIECES):
        beside(own_row, i, i).start()

    load_q.wait()
    queries = dot(normed[...], wq_ref[...])
    for k in range(CHUNKS):
        m, first = place(k)
        rows = slice(m * TOKENS + first, m * TOKENS + first + ROWS)
        for h in range(2):
            part = queries[rows, h * HEAD_DIM : (h + 1) * HEAD_DIM]
            q_hat[k, h * ROWS : (h + 1) * ROWS, :] = part
            q_low[k, h * ROWS : (h + 1) * ROWS, :] = part.astype(BF16)
    for b in range(WIDTH // BLOCK):
        rows = slice(b * BLOCK, (b + 1) * BLOCK)
        wc[:BLOCK, rows] = wq_ref[rows, :].T
    load_o.wait()
    for i in range(8):
        for half, b in enumerate(slice_blocks(i)):
            first = (2 * i + half) * BLOCK
            wot[first : first + BLOCK, :] = wo_ref[:, b * BLOCK : (b + 1) * BLOCK].T
    dkv_acc[...] = jnp.zeros_like(dkv_acc)

    @pl.when(top_section)
    def _():
        load_top.wait()
        for k in range(CHUNKS):
            m, first = place(k)
            for i in range(8):
                for half, b in enumerate(slice_blocks(i)):
                    g_buf[k, i, :, half * BLOCK : (half + 1) * BLOCK] = top_ref[
                        m, first : first + ROWS, b * BLOCK : (b + 1) * BLOCK
                    ]

    for copy in kvt_copies:
        copy.wait_recv()
    keyval = kvt[...].T
    for m in range(MICRO):
        rows = slice(m * TOKENS, (m + 1) * TOKENS)
        k_t[m] = kvt[:HEAD_DIM, rows]
        v_t[m] = kvt[HEAD_DIM:, rows]
        k_low[m] = keyval[rows, :HEAD_DIM]
        v_low[m] = keyval[rows, HEAD_DIM:]
    for k in range(CHUNKS):
        m, first = place(k)
        scores = dot(q_low[k], k_t[m]) * SCALE
        row = lax.rem(lax.broadcasted_iota(jnp.int32, scores.shape, 0), ROWS) + first
        scores = jnp.where(row >= lax.broadcasted_iota(jnp.int32, scores.shape, 1), scores, -1e30)
        scores = jnp.exp(scores - jnp.max(scores, axis=-1, keepdims=True))
        probs = scores / jnp.sum(scores, axis=-1, keepdims=True)
        p_buf[k] = probs
        p_low_t[k] = probs.T.astype(BF16)
        attended = dot(probs.astype(BF16), v_low[m]).astype(BF16)
        for h in range(2):
            att[k, :, h * HEAD_DIM : (h + 1) * HEAD_DIM] = attended[h * ROWS : (h + 1) * ROWS, :]

    @pl.when(s < SECTIONS - 4)
    def _():
        pl.semaphore_wait(gate, 1)
        for i in range(PIECES):
            across(own_row, i).start()

    for i in range(PIECES):
        across(far_row, i).wait_recv()
        beside(far_row, i, PIECES + i).start()

    @pl.when(s >= 4)
    def _():
        pl.semaphore_signal(gate, inc=1, device_id=(s - 4, d), device_id_type=MESH)

    for i in range(PIECES):
        beside(near_row, i, i).wait_recv()
        beside(cross_row, i, PIECES + i).wait_recv()

    own_slice = x_pos * 2 + c_pos

    def ag_copy(k, dx, dc):
        return remote(
            ag_buf.at[k], g_buf.at[k, own_slice], ag_send.at[k], ag_recv.at[k],
            s - 1, peer(dx, 0, dc),
        )

    def first_half(k):
        m, first = place(k)
        first = pl.multiple_of(first, ROWS)

        @pl.when(s < SECTIONS - 1)
        def _():
            all_of(g_buf.at[k], ag_recv.at[k]).wait()

        g = jnp.concatenate([g_buf[k, i] for i in range(8)], axis=1)
        og = dot(g, wot[...]).astype(BF16)
        og = jnp.concatenate([og[:, :HEAD_DIM], og[:, HEAD_DIM:]], axis=0)
        prob_grad = dot(og, v_t[m])
        probs = p_buf[k]
        delta = jnp.sum(probs * prob_grad, axis=-1, keepdims=True)
        score_grad = (probs * (prob_grad - delta)).astype(BF16)
        dq = (dot(score_grad, k_low[m]) * SCALE).astype(BF16)
        dkv_acc[m, :, :HEAD_DIM] += dot(score_grad, q_low[k], 0, 0) * SCALE
        dkv_acc[m, :, HEAD_DIM:] += dot(p_low_t[k], og)
        dkv = dkv_acc[m, pl.ds(first, ROWS), :].astype(BF16)
        keyval = jnp.concatenate(
            [k_low[m, pl.ds(first, ROWS), :], v_low[m, pl.ds(first, ROWS), :]], axis=1
        )
        stat = jnp.sum(dq.astype(F32) * q_hat[k], axis=-1, keepdims=True)
        stat = stat[:ROWS] + stat[ROWS:]
        stat += jnp.sum(dkv.astype(F32) * keyval.astype(F32), axis=-1, keepdims=True)
        r = r_buf[m, pl.ds(first, ROWS), :]
        stat = stat * (r * r / WIDTH)
        grads = jnp.concatenate([dq[:ROWS], dq[ROWS:], dkv], axis=1)

        def contribution(dx, dc):
            parts = []
            for half in range(2):
                block = columns((x_pos + dx) % 4 * 4 + half * 2 + (c_pos + dc) % 2)
                part = dot(grads, wc[:, block]) * (r * gain_ref[:, block].astype(F32))
                parts.append(part - x_ref[m, pl.ds(first, ROWS), block].astype(F32) * stat)
            return jnp.concatenate(parts, axis=1)

        for j, dx in enumerate(HOPS):
            near_out[k, j] = contribution(dx, 1).astype(BF16)
            remote(
                near_out.at[k, j], near_in.at[k, j], near_send.at[k], near_recv.at[k, j],
                s, peer(0, 0, 1),
            ).start()
        own = [contribution(dx, 0) for dx in HOPS]
        g_out[k] = g_buf[k]
        for j, dx in enumerate(HOPS):
            all_of(near_in.at[k, j], near_recv.at[k, j]).wait()
            part_buf[k, j] = (own[j] + near_in[k, j].astype(F32)).astype(BF16)
            for dz in (1, 0):
                if (dx, dz) == (0, 0):
                    continue
                remote(
                    part_buf.at[k, j], rs_buf.at[k, PEERS.index((dx, dz))],
                    rs_send.at[k], rs_recv.at[k], s, peer(dx, dz, 0),
                ).start()

    def second_half(k):
        m, first = place(k)
        first = pl.multiple_of(first, ROWS)
        total = g_buf[k, own_slice].astype(F32) + part_buf[k, len(HOPS) - 1].astype(F32)
        all_of(rs_buf.at[k], rs_recv.at[k]).wait()
        for j in range(len(PEERS)):
            total += rs_buf[k, j].astype(F32)
        result = total.astype(BF16)
        ag_buf[k] = result

        @pl.when(s > 0)
        def _():
            for dx in HOPS:
                for dc in (1, 0):
                    ag_copy(k, dx, dc).start()

        out_ref[m, pl.ds(first, ROWS), :] = jnp.where(
            z_pos == 0, result[:, :BLOCK], result[:, BLOCK:]
        )

    def step(k, carry):
        @pl.when(k < CHUNKS)
        def _():
            first_half(k)

        @pl.when(k >= LAG)
        def _():
            second_half(k - LAG)

        return carry

    lax.fori_loop(0, CHUNKS + LAG, step, 0)

    for copy in kvt_copies:
        copy.wait_send()
    for i in range(PIECES):
        across(own_row, i).wait_send()
        beside(own_row, i, i).wait_send()
        beside(far_row, i, PIECES + i).wait_send()

    def drain(k, carry):
        all_of(near_in.at[k], near_send.at[k]).wait()
        all_of(rs_buf.at[k], rs_send.at[k]).wait()

        @pl.when(s > 0)
        def _():
            all_of(g_buf.at[k], ag_send.at[k]).wait()

        return carry

    lax.fori_loop(0, CHUNKS, drain, 0)


def relay(x, top, wq, wkv, wo, gain):
    vmem = pl.BlockSpec(memory_space=pltpu.VMEM)
    hbm = pl.BlockSpec(memory_space=pl.ANY)
    dma = pltpu.SemaphoreType.DMA
    return pl.pallas_call(
        kernel,
        out_shape=(
            jax.ShapeDtypeStruct((MICRO, TOKENS, BLOCK), BF16),
            jax.ShapeDtypeStruct((CHUNKS, ROWS, BLOCK), BF16),
            jax.ShapeDtypeStruct((CHUNKS, 8, ROWS, SLICE), BF16),
        ),
        in_specs=[hbm] * 5 + [vmem],
        out_specs=(vmem, vmem, vmem),
        scratch_shapes=[
            pltpu.VMEM((MICRO, TOKENS, WIDTH), BF16),
            pltpu.VMEM((MICRO, TOKENS, WIDTH), BF16),
            pltpu.VMEM((WIDTH, BLOCK), BF16),
            pltpu.VMEM((BLOCK, WIDTH), BF16),
            pltpu.VMEM((2 * BLOCK, WIDTH), BF16),
            pltpu.VMEM((WIDTH, BLOCK), BF16),
            pltpu.VMEM((MICRO * TOKENS, WIDTH), BF16),
            pltpu.VMEM((MICRO, TOKENS, 1), F32),
            pltpu.VMEM((CHUNKS, 2 * ROWS, HEAD_DIM), F32),
            pltpu.VMEM((CHUNKS, 2 * ROWS, HEAD_DIM), BF16),
            pltpu.VMEM((BLOCK, MICRO * TOKENS), BF16),
            pltpu.VMEM((MICRO, HEAD_DIM, TOKENS), BF16),
            pltpu.VMEM((MICRO, HEAD_DIM, TOKENS), BF16),
            pltpu.VMEM((MICRO, TOKENS, HEAD_DIM), BF16),
            pltpu.VMEM((MICRO, TOKENS, HEAD_DIM), BF16),
            pltpu.VMEM((CHUNKS, 2 * ROWS, TOKENS), F32),
            pltpu.VMEM((CHUNKS, TOKENS, 2 * ROWS), BF16),
            pltpu.VMEM((MICRO, TOKENS, BLOCK), F32),
            pltpu.VMEM((CHUNKS, 8, ROWS, SLICE), BF16),
            pltpu.VMEM((CHUNKS, len(HOPS), ROWS, SLICE), BF16),
            pltpu.VMEM((CHUNKS, len(HOPS), ROWS, SLICE), BF16),
            pltpu.VMEM((CHUNKS, len(HOPS), ROWS, SLICE), BF16),
            pltpu.VMEM((CHUNKS, len(PEERS), ROWS, SLICE), BF16),
            pltpu.VMEM((CHUNKS, ROWS, SLICE), BF16),
            dma((5,)),
            dma((CHUNKS,)),
            dma((CHUNKS, len(HOPS))),
            dma((CHUNKS,)),
            dma((CHUNKS,)),
            dma((CHUNKS,)),
            dma((CHUNKS,)),
            dma((3,)),
            dma((3,)),
            dma((PIECES,)),
            dma((PIECES,)),
            dma((2 * PIECES,)),
            dma((2 * PIECES,)),
            pltpu.SemaphoreType.REGULAR,
        ],
        compiler_params=pltpu.CompilerParams(
            collective_id=0, has_side_effects=True, vmem_limit_bytes=60 * 1024 * 1024
        ),
        name="relay",
    )(x, top, wq, wkv, wo, gain)


def weight_kernel(block_ref, att_ref, g_ref, grad_ref):
    attended = att_ref[...].reshape(CHUNKS * ROWS, BLOCK)
    scale = block_ref[0].astype(F32)
    for core in range(2):
        g = g_ref[:, core].reshape(CHUNKS * ROWS, SLICE)
        part = dot(attended, g, 0, 0) * scale
        for half in range(2):
            first = (half * 2 + core) * BLOCK
            grad_ref[:, first : first + BLOCK] = part[:, half * BLOCK : (half + 1) * BLOCK]


def weight_grad(new_block, att, g):
    return pl.pallas_call(
        weight_kernel,
        out_shape=jax.ShapeDtypeStruct((BLOCK, WIDTH), F32),
        grid=(4,),
        in_specs=[
            pl.BlockSpec(memory_space=pltpu.SMEM),
            pl.BlockSpec((CHUNKS, ROWS, BLOCK), lambda i: (0, 0, 0)),
            pl.BlockSpec((CHUNKS, 2, ROWS, SLICE), lambda i: (0, i, 0, 0)),
        ],
        out_specs=pl.BlockSpec((BLOCK, 4 * BLOCK), lambda i: (0, i)),
        compiler_params=pltpu.CompilerParams(vmem_limit_bytes=16 * 1024 * 1024),
        name="weight_grad",
    )(new_block, att, g)


def body(layer_inputs, top_grad, w_query, w_keyval, w_out, norm_gain, new_block):
    stream, att, g = relay(
        layer_inputs[0], top_grad, w_query[0], w_keyval[0].T, w_out[0], norm_gain
    )
    return stream[None], weight_grad(new_block, att, g)[None]


def solution(mesh):
    in_specs = (
        P("section", None, None, None),
        P(),
        P("section", None, "dp"),
        P("section", None, "dp"),
        P("section", "dp", None),
        P("section", None),
        P("section"),
    )
    out_specs = (P("section", None, None, "dp"), P("section", "dp", None))
    return jax.shard_map(body, mesh=mesh, in_specs=in_specs, out_specs=out_specs, check_vma=False)
```

```python
import jax
import jax.numpy as jnp
from jax import lax
from jax.experimental import pallas as pl
from jax.experimental.pallas import tpu as pltpu
from jax.sharding import PartitionSpec as P

HEAD_DIM = 128
EPS = 1e-05
MESH = pl.DeviceIdType.MESH
F32 = jnp.float32
BF16 = jnp.bfloat16

SECTIONS = 16
TOKENS = 64
MICRO = 2
WIDTH = 4096
ROWS = 16
PARTS = TOKENS // ROWS
CHUNKS = PARTS
LAG = 1
BLOCK = 256
SLICE = 4 * BLOCK
HEADS = 4
KV_ROW = HEADS * HEAD_DIM
SCALE = HEAD_DIM ** (-0.5)

HOPS = (2, 1, 3, 0)
PEERS = [(dx, dz) for dx in HOPS for dz in (1, 0)][:-1]
PIECES = 8


def dot(a, b, ca=1, cb=0):
    return lax.dot_general(a, b, (((ca,), (cb,)), ((), ())), preferred_element_type=F32)


def first_token(k):
    return (PARTS - 1 - k) * ROWS


def heads_to_rows(value):
    return jnp.concatenate(
        [value[:, h * HEAD_DIM : (h + 1) * HEAD_DIM] for h in range(HEADS)], axis=0
    )


def rows_to_heads(value):
    return jnp.concatenate([value[h * ROWS : (h + 1) * ROWS] for h in range(HEADS)], axis=1)


def kernel(
    x_hbm, top_hbm, wq_hbm, wkv_hbm, wo_hbm, gain_ref,
    out_ref, att_out, g_out,
    x_ref, top_ref, wq_ref, wo_ref,
    wc, wot, normed, r_buf, q_hat, q_low, kvt, k_t, v_t, k_low, v_low, p_buf, p_low_t, dkv_acc,
    g_buf, g_in, att_own, att_send, att_in, part_buf, rs_buf, ag_buf, side_buf, side_in,
    load_sem, rs_send, rs_recv, ag_send, ag_recv, w_send, w_recv, g_send, g_recv,
    side_send, side_recv, att_sem, kv_send, kv_recv, far_send, far_recv, pass_send, pass_recv, gate,
):
    s = lax.axis_index("section")
    d = lax.axis_index("dp")
    x_pos = d // 4
    z_pos = d // 2 % 2
    c_pos = d % 2
    other = 1 - c_pos
    top_section = s == SECTIONS - 1

    def peer(dx, dz, dc):
        return (x_pos + dx) % 4 * 4 + (z_pos + dz) % 2 * 2 + (c_pos + dc) % 2

    def all_of(ref, sem):
        return pltpu.make_async_copy(ref, ref, sem)

    def remote(src, dst, send, recv, section, device):
        return pltpu.make_async_remote_copy(
            src_ref=src, dst_ref=dst, send_sem=send, recv_sem=recv,
            device_id=(section, device), device_id_type=MESH,
        )

    own_row = pl.multiple_of((z_pos * 2 + c_pos) * 64, 64)
    near_row = pl.multiple_of((z_pos * 2 + 1 - c_pos) * 64, 64)
    far_row = pl.multiple_of(((1 - z_pos) * 2 + c_pos) * 64, 64)
    cross_row = pl.multiple_of(((1 - z_pos) * 2 + 1 - c_pos) * 64, 64)

    def wc_rows(row):
        return wc.at[pl.ds(pl.multiple_of(KV_ROW + row, 64), 64)]

    load_x = pltpu.make_async_copy(x_hbm, x_ref, load_sem.at[0])
    load_kv = pltpu.make_async_copy(wkv_hbm, wc_rows(own_row), load_sem.at[1])
    load_q = pltpu.make_async_copy(wq_hbm, wq_ref.at[c_pos], load_sem.at[2])
    load_o = pltpu.make_async_copy(wo_hbm, wo_ref.at[c_pos], load_sem.at[3])
    load_top = pltpu.make_async_copy(top_hbm, top_ref, load_sem.at[4])
    for load in (load_kv, load_x, load_q, load_o):
        load.start()

    @pl.when(top_section)
    def _():
        load_top.start()

    barrier = pltpu.get_barrier_semaphore()

    def greet(section, device):
        pl.semaphore_signal(barrier, inc=1, device_id=(section, device), device_id_type=MESH)

    for dx, dz in PEERS:
        greet(s, peer(dx, dz, 0))
    greet(s, peer(0, 0, 1))
    greet(s, peer(0, 1, 1))

    @pl.when(s > 0)
    def _():
        for dx in HOPS:
            greet(s - 1, peer(dx, 0, 0))

    @pl.when(s < SECTIONS - 1)
    def _():
        for dx in HOPS:
            greet(s + 1, peer(dx, 0, 0))

    @pl.when(s < SECTIONS - 4)
    def _():
        greet(s + 4, d)

    greetings = (
        len(PEERS) + 2
        + jnp.where(s > 0, len(HOPS), 0)
        + jnp.where(s < SECTIONS - 1, len(HOPS), 0)
        + jnp.where(s >= 4, 1, 0)
    )
    pl.semaphore_wait(barrier, greetings)
    load_kv.wait()

    def piece(row, i):
        width = WIDTH // PIECES
        return wc.at[pl.ds(pl.multiple_of(KV_ROW + row, 64), 64), pl.ds(i * width, width)]

    def across(row, i):
        part = piece(row, i)
        return remote(part, part, far_send.at[i], far_recv.at[i], s, peer(0, 1, 0))

    def beside(row, i, sem):
        part = piece(row, i)
        return remote(part, part, pass_send.at[sem], pass_recv.at[sem], s, peer(0, 0, 1))

    @pl.when(s >= SECTIONS - 4)
    def _():
        for i in range(PIECES):
            across(own_row, i).start()

    share_q = remote(wq_hbm, wq_ref.at[c_pos], w_send.at[0], w_recv.at[0], s, peer(0, 0, 1))
    share_o = remote(wo_hbm, wo_ref.at[c_pos], w_send.at[1], w_recv.at[1], s, peer(0, 0, 1))
    share_q.start()
    share_o.start()
    for i in range(PIECES):
        beside(own_row, i, i).start()

    load_x.wait()
    for m in range(MICRO):
        for first in range(0, TOKENS, ROWS):
            xf = x_ref[m, first : first + ROWS, :].astype(F32)
            r = lax.rsqrt(jnp.mean(xf * xf, axis=-1, keepdims=True) + EPS)
            r_buf[m, first : first + ROWS, :] = r
            normed[m, first : first + ROWS, :] = (xf * r * gain_ref[...].astype(F32)).astype(BF16)
    tokens = normed[...].reshape(MICRO * TOKENS, WIDTH)
    kvt[pl.ds(own_row, 64), :] = dot(wc[pl.ds(KV_ROW + own_row, 64), :], tokens, 1, 1).astype(BF16)

    own_kvt = kvt.at[pl.ds(own_row, 64)]
    kvt_copies = [
        remote(own_kvt, own_kvt, kv_send.at[i], kv_recv.at[i], s, peer(0, dz, dc))
        for i, (dz, dc) in enumerate([(1, 0), (1, 1), (0, 1)])
    ]
    for copy in kvt_copies:
        copy.start()

    load_q.wait()
    share_q.wait_recv()
    for half in range(2):
        queries = dot(normed[c_pos], wq_ref[half])
        for k in range(CHUNKS):
            first = first_token(k)
            for h in range(2):
                part = queries[first : first + ROWS, h * HEAD_DIM : (h + 1) * HEAD_DIM]
                row = (2 * half + h) * ROWS
                q_hat[k, row : row + ROWS, :] = part
                q_low[k, row : row + ROWS, :] = part.astype(BF16)
        for b in range(WIDTH // BLOCK):
            rows = slice(b * BLOCK, (b + 1) * BLOCK)
            wc[half * BLOCK : (half + 1) * BLOCK, rows] = wq_ref[half, rows, :].T
    dkv_acc[...] = jnp.zeros_like(dkv_acc)

    @pl.when(top_section)
    def _():
        load_top.wait()
        for k in range(CHUNKS):
            first = first_token(k)
            for i in range(4):
                g_buf[k, i] = top_ref[c_pos, first : first + ROWS, i * SLICE : (i + 1) * SLICE]

    for copy in kvt_copies:
        copy.wait_recv()
    keyval = kvt[...].T

    def pick(first_micro, second_micro):
        return jnp.where(c_pos == 0, first_micro.astype(F32), second_micro.astype(F32)).astype(BF16)

    mine = pick(kvt[:, :TOKENS], kvt[:, TOKENS:])
    k_t[...] = mine[:HEAD_DIM]
    v_t[...] = mine[HEAD_DIM:]
    mine = pick(keyval[:TOKENS], keyval[TOKENS:])
    k_low[...] = mine[:, :HEAD_DIM]
    v_low[...] = mine[:, HEAD_DIM:]
    for k in range(CHUNKS):
        first = first_token(k)
        scores = dot(q_low[k], k_t[...]) * SCALE
        row = lax.rem(lax.broadcasted_iota(jnp.int32, scores.shape, 0), ROWS) + first
        scores = jnp.where(row >= lax.broadcasted_iota(jnp.int32, scores.shape, 1), scores, -1e30)
        scores = jnp.exp(scores - jnp.max(scores, axis=-1, keepdims=True))
        probs = scores / jnp.sum(scores, axis=-1, keepdims=True)
        p_buf[k] = probs
        p_low_t[k] = probs.T.astype(BF16)
        attended = rows_to_heads(dot(probs.astype(BF16), v_low[...]))
        left, right = attended[:, :BLOCK], attended[:, BLOCK:]
        att_own[k] = jnp.where(c_pos == 0, left, right).astype(BF16)
        att_send[k] = jnp.where(c_pos == 0, right, left).astype(BF16)
    share_att = remote(att_send, att_in, att_sem.at[0], att_sem.at[1], s, peer(0, 0, 1))
    share_att.start()

    load_o.wait()
    share_o.wait_recv()
    for half in range(2):
        for b in range(WIDTH // BLOCK):
            rows = slice(b * BLOCK, (b + 1) * BLOCK)
            wot[rows, half * BLOCK : (half + 1) * BLOCK] = wo_ref[half, :, rows].T

    @pl.when(s < SECTIONS - 4)
    def _():
        pl.semaphore_wait(gate, 1)
        for i in range(PIECES):
            across(own_row, i).start()

    for i in range(PIECES):
        across(far_row, i).wait_recv()
        beside(far_row, i, PIECES + i).start()

    for i in range(PIECES):
        beside(near_row, i, i).wait_recv()
        beside(cross_row, i, PIECES + i).wait_recv()

    def ag_copy(k, dx):
        return remote(
            ag_buf.at[k], g_buf.at[k, x_pos], ag_send.at[k], ag_recv.at[k], s - 1, peer(dx, 0, 0)
        )

    def share_g(k):
        return remote(g_buf.at[k], g_in.at[k], g_send.at[k], g_recv.at[k], s, peer(0, 0, 1))

    def share_result(k):
        return remote(
            side_buf.at[k], side_in.at[k], side_send.at[k], side_recv.at[k], s, peer(0, 0, 1)
        )

    def first_half(k):
        first = pl.multiple_of(first_token(k), ROWS)

        @pl.when(s < SECTIONS - 1)
        def _():
            all_of(g_buf.at[k], ag_recv.at[k]).wait()

        g = jnp.concatenate([g_buf[k, i] for i in range(4)], axis=1)
        og = heads_to_rows(dot(g, wot[...]).astype(BF16))
        prob_grad = dot(og, v_t[...])
        probs = p_buf[k]
        delta = jnp.sum(probs * prob_grad, axis=-1, keepdims=True)
        score_grad = (probs * (prob_grad - delta)).astype(BF16)
        dq = (dot(score_grad, k_low[...]) * SCALE).astype(BF16)
        dkv_acc[:, :HEAD_DIM] += dot(score_grad, q_low[k], 0, 0) * SCALE
        dkv_acc[:, HEAD_DIM:] += dot(p_low_t[k], og)
        dkv = dkv_acc[pl.ds(first, ROWS), :].astype(BF16)
        keyval = jnp.concatenate(
            [k_low[pl.ds(first, ROWS), :], v_low[pl.ds(first, ROWS), :]], axis=1
        )
        stat = jnp.sum(rows_to_heads(dq.astype(F32) * q_hat[k]), axis=-1, keepdims=True)
        stat += jnp.sum(dkv.astype(F32) * keyval.astype(F32), axis=-1, keepdims=True)
        r = r_buf[c_pos, pl.ds(first, ROWS), :]
        stat = stat * (r * r / WIDTH)
        grads = jnp.concatenate([rows_to_heads(dq), dkv], axis=1)
        for j, dx in enumerate(HOPS):
            block = pl.ds(pl.multiple_of((x_pos + dx) % 4 * SLICE, SLICE), SLICE)
            part = dot(grads, wc[:, block]) * (r * gain_ref[:, block].astype(F32))
            part -= x_ref[c_pos, pl.ds(first, ROWS), block].astype(F32) * stat
            part_buf[k, j] = part.astype(BF16)
            for dz in (1, 0):
                if (dx, dz) == (0, 0):
                    continue
                remote(
                    part_buf.at[k, j], rs_buf.at[k, PEERS.index((dx, dz))],
                    rs_send.at[k], rs_recv.at[k], s, peer(dx, dz, 0),
                ).start()
        share_g(k).start()

    def second_half(k):
        first = pl.multiple_of(first_token(k), ROWS)
        total = g_buf[k, x_pos].astype(F32) + part_buf[k, len(HOPS) - 1].astype(F32)
        all_of(rs_buf.at[k], rs_recv.at[k]).wait()
        for j in range(len(PEERS)):
            total += rs_buf[k, j].astype(F32)
        ag_buf[k] = total.astype(BF16)

        @pl.when(s > 0)
        def _():
            for dx in HOPS:
                ag_copy(k, dx).start()

        half = jnp.where(z_pos == 0, total[:, : 2 * BLOCK], total[:, 2 * BLOCK :])
        left, right = half[:, :BLOCK], half[:, BLOCK:]
        side_buf[k] = jnp.where(c_pos == 0, right, left).astype(BF16)
        share_result(k).start()
        out_ref[c_pos, pl.ds(first, ROWS), :] = jnp.where(c_pos == 0, left, right).astype(BF16)

    def step(k, carry):
        @pl.when(k < CHUNKS)
        def _():
            first_half(k)

        @pl.when(k >= LAG)
        def _():
            second_half(k - LAG)

        return carry

    lax.fori_loop(0, CHUNKS + LAG, step, 0)

    @pl.when(s >= 4)
    def _():
        pl.semaphore_signal(gate, inc=1, device_id=(s - 4, d), device_id_type=MESH)

    share_att.wait_recv()
    att_out[c_pos] = att_own[...]
    att_out[other] = att_in[...]
    g_out[c_pos] = g_buf[...]
    for k in range(CHUNKS):
        share_g(k).wait_recv()
        g_out[other, k] = g_in[k]
    for k in range(CHUNKS):
        first = first_token(k)
        share_result(k).wait_recv()
        out_ref[other, first : first + ROWS, :] = side_in[k]

    for copy in (*kvt_copies, share_q, share_o, share_att):
        copy.wait_send()
    for i in range(PIECES):
        across(own_row, i).wait_send()
        beside(own_row, i, i).wait_send()
        beside(far_row, i, PIECES + i).wait_send()

    def drain(k, carry):
        all_of(rs_buf.at[k], rs_send.at[k]).wait()
        share_g(k).wait_send()
        share_result(k).wait_send()

        @pl.when(s > 0)
        def _():
            all_of(g_buf.at[k], ag_send.at[k]).wait()

        return carry

    lax.fori_loop(0, CHUNKS, drain, 0)


def relay(x, top, wq, wkv, wo, gain):
    vmem = pl.BlockSpec(memory_space=pltpu.VMEM)
    hbm = pl.BlockSpec(memory_space=pl.ANY)
    dma = pltpu.SemaphoreType.DMA
    return pl.pallas_call(
        kernel,
        out_shape=(
            jax.ShapeDtypeStruct((MICRO, TOKENS, BLOCK), BF16),
            jax.ShapeDtypeStruct((MICRO, CHUNKS, ROWS, BLOCK), BF16),
            jax.ShapeDtypeStruct((MICRO, CHUNKS, 4, ROWS, SLICE), BF16),
        ),
        in_specs=[hbm] * 5 + [vmem],
        out_specs=(vmem, vmem, vmem),
        scratch_shapes=[
            pltpu.VMEM((MICRO, TOKENS, WIDTH), BF16),
            pltpu.VMEM((MICRO, TOKENS, WIDTH), BF16),
            pltpu.VMEM((2, WIDTH, BLOCK), BF16),
            pltpu.VMEM((2, BLOCK, WIDTH), BF16),
            pltpu.VMEM((KV_ROW + BLOCK, WIDTH), BF16),
            pltpu.VMEM((WIDTH, KV_ROW), BF16),
            pltpu.VMEM((MICRO, TOKENS, WIDTH), BF16),
            pltpu.VMEM((MICRO, TOKENS, 1), F32),
            pltpu.VMEM((CHUNKS, HEADS * ROWS, HEAD_DIM), F32),
            pltpu.VMEM((CHUNKS, HEADS * ROWS, HEAD_DIM), BF16),
            pltpu.VMEM((BLOCK, MICRO * TOKENS), BF16),
            pltpu.VMEM((HEAD_DIM, TOKENS), BF16),
            pltpu.VMEM((HEAD_DIM, TOKENS), BF16),
            pltpu.VMEM((TOKENS, HEAD_DIM), BF16),
            pltpu.VMEM((TOKENS, HEAD_DIM), BF16),
            pltpu.VMEM((CHUNKS, HEADS * ROWS, TOKENS), F32),
            pltpu.VMEM((CHUNKS, TOKENS, HEADS * ROWS), BF16),
            pltpu.VMEM((TOKENS, BLOCK), F32),
            pltpu.VMEM((CHUNKS, 4, ROWS, SLICE), BF16),
            pltpu.VMEM((CHUNKS, 4, ROWS, SLICE), BF16),
            pltpu.VMEM((CHUNKS, ROWS, BLOCK), BF16),
            pltpu.VMEM((CHUNKS, ROWS, BLOCK), BF16),
            pltpu.VMEM((CHUNKS, ROWS, BLOCK), BF16),
            pltpu.VMEM((CHUNKS, len(HOPS), ROWS, SLICE), BF16),
            pltpu.VMEM((CHUNKS, len(PEERS), ROWS, SLICE), BF16),
            pltpu.VMEM((CHUNKS, ROWS, SLICE), BF16),
            pltpu.VMEM((CHUNKS, ROWS, BLOCK), BF16),
            pltpu.VMEM((CHUNKS, ROWS, BLOCK), BF16),
            dma((5,)),
            dma((CHUNKS,)),
            dma((CHUNKS,)),
            dma((CHUNKS,)),
            dma((CHUNKS,)),
            dma((2,)),
            dma((2,)),
            dma((CHUNKS,)),
            dma((CHUNKS,)),
            dma((CHUNKS,)),
            dma((CHUNKS,)),
            dma((2,)),
            dma((3,)),
            dma((3,)),
            dma((PIECES,)),
            dma((PIECES,)),
            dma((2 * PIECES,)),
            dma((2 * PIECES,)),
            pltpu.SemaphoreType.REGULAR,
        ],
        compiler_params=pltpu.CompilerParams(
            collective_id=0, has_side_effects=True, vmem_limit_bytes=60 * 1024 * 1024
        ),
        name="relay",
    )(x, top, wq, wkv, wo, gain)


def weight_kernel(block_ref, att_ref, g_ref, grad_ref):
    attended = att_ref[...].reshape(MICRO * TOKENS, BLOCK)
    g = g_ref[...].reshape(MICRO * TOKENS, SLICE)
    grad_ref[...] = dot(attended, g, 0, 0) * block_ref[0].astype(F32)


def weight_grad(new_block, att, g):
    return pl.pallas_call(
        weight_kernel,
        out_shape=jax.ShapeDtypeStruct((BLOCK, WIDTH), F32),
        grid=(4,),
        in_specs=[
            pl.BlockSpec(memory_space=pltpu.SMEM),
            pl.BlockSpec((MICRO, CHUNKS, ROWS, BLOCK), lambda i: (0, 0, 0, 0)),
            pl.BlockSpec((MICRO, CHUNKS, 1, ROWS, SLICE), lambda i: (0, 0, i, 0, 0)),
        ],
        out_specs=pl.BlockSpec((BLOCK, SLICE), lambda i: (0, i)),
        compiler_params=pltpu.CompilerParams(vmem_limit_bytes=16 * 1024 * 1024),
        name="weight_grad",
    )(new_block, att, g)


def body(layer_inputs, top_grad, w_query, w_keyval, w_out, norm_gain, new_block):
    stream, att, g = relay(
        layer_inputs[0], top_grad, w_query[0], w_keyval[0].T, w_out[0], norm_gain
    )
    return stream[None], weight_grad(new_block, att, g)[None]


def solution(mesh):
    in_specs = (
        P("section", None, None, None),
        P(),
        P("section", None, "dp"),
        P("section", None, "dp"),
        P("section", "dp", None),
        P("section", None),
        P("section"),
    )
    out_specs = (P("section", None, None, "dp"), P("section", "dp", None))
    return jax.shard_map(body, mesh=mesh, in_specs=in_specs, out_specs=out_specs, check_vma=False)
```

```python
import jax
import jax.numpy as jnp
from jax import lax
from jax.experimental import pallas as pl
from jax.experimental.pallas import tpu as pltpu
from jax.sharding import PartitionSpec as P

HEAD_DIM = 128
EPS = 1e-05
MESH = pl.DeviceIdType.MESH
F32 = jnp.float32
BF16 = jnp.bfloat16

SECTIONS = 16
TOKENS = 64
MICRO = 2
WIDTH = 4096
ROWS = 16
PARTS = TOKENS // ROWS
CHUNKS = PARTS
LAG = 1
BLOCK = 256
SLICE = 4 * BLOCK
HEADS = 4
KV_ROW = HEADS * HEAD_DIM
SCALE = HEAD_DIM ** (-0.5)

HOPS = (2, 1, 3, 0)
PEERS = [(dx, dz) for dx in HOPS for dz in (1, 0)][:-1]
PIECES = 8


def dot(a, b, ca=1, cb=0):
    return lax.dot_general(a, b, (((ca,), (cb,)), ((), ())), preferred_element_type=F32)


def first_token(k):
    return (PARTS - 1 - k) * ROWS


def heads_to_rows(value):
    return jnp.concatenate(
        [value[:, h * HEAD_DIM : (h + 1) * HEAD_DIM] for h in range(HEADS)], axis=0
    )


def rows_to_heads(value):
    return jnp.concatenate([value[h * ROWS : (h + 1) * ROWS] for h in range(HEADS)], axis=1)


def kernel(
    x_hbm, top_hbm, wq_hbm, wkv_hbm, wo_hbm, gain_ref,
    out_ref, att_out, g_out,
    x_ref, top_ref, wq_ref, wo_ref,
    wc, wot, normed, r_buf, q_hat, q_low, kvt, k_t, v_t, k_low, v_low, p_buf, p_low_t, dkv_acc,
    g_buf, g_in, att_own, att_send, att_in, part_buf, rs_buf, ag_buf, side_buf, side_in,
    load_sem, rs_send, rs_recv, ag_send, ag_recv, w_send, w_recv, g_send, g_recv,
    side_send, side_recv, att_sem, kv_send, kv_recv, far_send, far_recv, pass_send, pass_recv, gate,
):
    s = lax.axis_index("section")
    d = lax.axis_index("dp")
    x_pos = d // 4
    z_pos = d // 2 % 2
    c_pos = d % 2
    other = 1 - c_pos
    top_section = s == SECTIONS - 1

    def peer(dx, dz, dc):
        return (x_pos + dx) % 4 * 4 + (z_pos + dz) % 2 * 2 + (c_pos + dc) % 2

    def all_of(ref, sem):
        return pltpu.make_async_copy(ref, ref, sem)

    def remote(src, dst, send, recv, section, device):
        return pltpu.make_async_remote_copy(
            src_ref=src, dst_ref=dst, send_sem=send, recv_sem=recv,
            device_id=(section, device), device_id_type=MESH,
        )

    own_row = pl.multiple_of((z_pos * 2 + c_pos) * 64, 64)
    near_row = pl.multiple_of((z_pos * 2 + 1 - c_pos) * 64, 64)
    far_row = pl.multiple_of(((1 - z_pos) * 2 + c_pos) * 64, 64)
    cross_row = pl.multiple_of(((1 - z_pos) * 2 + 1 - c_pos) * 64, 64)

    def wc_rows(row):
        return wc.at[pl.ds(pl.multiple_of(KV_ROW + row, 64), 64)]

    load_x = pltpu.make_async_copy(x_hbm, x_ref, load_sem.at[0])
    load_kv = pltpu.make_async_copy(wkv_hbm, wc_rows(own_row), load_sem.at[1])
    load_q = pltpu.make_async_copy(wq_hbm, wq_ref.at[c_pos], load_sem.at[2])
    load_o = pltpu.make_async_copy(wo_hbm, wo_ref.at[c_pos], load_sem.at[3])
    load_top = pltpu.make_async_copy(top_hbm, top_ref, load_sem.at[4])
    for load in (load_kv, load_x, load_q, load_o):
        load.start()

    @pl.when(top_section)
    def _():
        load_top.start()

    barrier = pltpu.get_barrier_semaphore()

    def greet(section, device):
        pl.semaphore_signal(barrier, inc=1, device_id=(section, device), device_id_type=MESH)

    for dx, dz in PEERS:
        greet(s, peer(dx, dz, 0))
    greet(s, peer(0, 0, 1))
    greet(s, peer(0, 1, 1))

    @pl.when(s > 0)
    def _():
        for dx in HOPS:
            greet(s - 1, peer(dx, 0, 0))

    @pl.when(s < SECTIONS - 1)
    def _():
        for dx in HOPS:
            greet(s + 1, peer(dx, 0, 0))

    @pl.when(s < SECTIONS - 4)
    def _():
        greet(s + 4, d)

    greetings = (
        len(PEERS) + 2
        + jnp.where(s > 0, len(HOPS), 0)
        + jnp.where(s < SECTIONS - 1, len(HOPS), 0)
        + jnp.where(s >= 4, 1, 0)
    )
    pl.semaphore_wait(barrier, greetings)
    load_kv.wait()

    def piece(row, i):
        width = WIDTH // PIECES
        return wc.at[pl.ds(pl.multiple_of(KV_ROW + row, 64), 64), pl.ds(i * width, width)]

    def across(row, i):
        part = piece(row, i)
        return remote(part, part, far_send.at[i], far_recv.at[i], s, peer(0, 1, 0))

    def beside(row, i, sem):
        part = piece(row, i)
        return remote(part, part, pass_send.at[sem], pass_recv.at[sem], s, peer(0, 0, 1))

    @pl.when(s >= SECTIONS - 4)
    def _():
        for i in range(PIECES):
            across(own_row, i).start()

    share_q = remote(wq_hbm, wq_ref.at[c_pos], w_send.at[0], w_recv.at[0], s, peer(0, 0, 1))
    share_o = remote(wo_hbm, wo_ref.at[c_pos], w_send.at[1], w_recv.at[1], s, peer(0, 0, 1))
    share_q.start()
    share_o.start()
    for i in range(PIECES):
        beside(own_row, i, i).start()

    load_x.wait()
    for m in range(MICRO):
        for first in range(0, TOKENS, ROWS):
            xf = x_ref[m, first : first + ROWS, :].astype(F32)
            r = lax.rsqrt(jnp.mean(xf * xf, axis=-1, keepdims=True) + EPS)
            r_buf[m, first : first + ROWS, :] = r
            normed[m, first : first + ROWS, :] = (xf * r * gain_ref[...].astype(F32)).astype(BF16)
    tokens = normed[...].reshape(MICRO * TOKENS, WIDTH)
    kvt[pl.ds(own_row, 64), :] = dot(wc[pl.ds(KV_ROW + own_row, 64), :], tokens, 1, 1).astype(BF16)

    own_kvt = kvt.at[pl.ds(own_row, 64)]
    kvt_copies = [
        remote(own_kvt, own_kvt, kv_send.at[i], kv_recv.at[i], s, peer(0, dz, dc))
        for i, (dz, dc) in enumerate([(1, 0), (1, 1), (0, 1)])
    ]
    for copy in kvt_copies:
        copy.start()

    load_q.wait()
    share_q.wait_recv()
    for half in range(2):
        queries = dot(normed[c_pos], wq_ref[half])
        for k in range(CHUNKS):
            first = first_token(k)
            for h in range(2):
                part = queries[first : first + ROWS, h * HEAD_DIM : (h + 1) * HEAD_DIM]
                row = (2 * half + h) * ROWS
                q_hat[k, row : row + ROWS, :] = part
                q_low[k, row : row + ROWS, :] = part.astype(BF16)
        for b in range(WIDTH // BLOCK):
            rows = slice(b * BLOCK, (b + 1) * BLOCK)
            wc[half * BLOCK : (half + 1) * BLOCK, rows] = wq_ref[half, rows, :].T
    dkv_acc[...] = jnp.zeros_like(dkv_acc)

    @pl.when(top_section)
    def _():
        load_top.wait()
        for k in range(CHUNKS):
            first = first_token(k)
            for i in range(4):
                g_buf[k, i] = top_ref[c_pos, first : first + ROWS, i * SLICE : (i + 1) * SLICE]

    for copy in kvt_copies:
        copy.wait_recv()
    keyval = kvt[...].T

    def pick(first_micro, second_micro):
        return jnp.where(c_pos == 0, first_micro.astype(F32), second_micro.astype(F32)).astype(BF16)

    mine = pick(kvt[:, :TOKENS], kvt[:, TOKENS:])
    k_t[...] = mine[:HEAD_DIM]
    v_t[...] = mine[HEAD_DIM:]
    mine = pick(keyval[:TOKENS], keyval[TOKENS:])
    k_low[...] = mine[:, :HEAD_DIM]
    v_low[...] = mine[:, HEAD_DIM:]
    for k in range(CHUNKS):
        first = first_token(k)
        scores = dot(q_low[k], k_t[...]) * SCALE
        row = lax.rem(lax.broadcasted_iota(jnp.int32, scores.shape, 0), ROWS) + first
        scores = jnp.where(row >= lax.broadcasted_iota(jnp.int32, scores.shape, 1), scores, -1e30)
        scores = jnp.exp(scores - jnp.max(scores, axis=-1, keepdims=True))
        probs = scores / jnp.sum(scores, axis=-1, keepdims=True)
        p_buf[k] = probs
        p_low_t[k] = probs.T.astype(BF16)
        attended = rows_to_heads(dot(probs.astype(BF16), v_low[...]))
        left, right = attended[:, :BLOCK], attended[:, BLOCK:]
        att_own[k] = jnp.where(c_pos == 0, left, right).astype(BF16)
        att_send[k] = jnp.where(c_pos == 0, right, left).astype(BF16)
    share_att = remote(att_send, att_in, att_sem.at[0], att_sem.at[1], s, peer(0, 0, 1))
    share_att.start()

    load_o.wait()
    share_o.wait_recv()
    for half in range(2):
        for b in range(WIDTH // BLOCK):
            rows = slice(b * BLOCK, (b + 1) * BLOCK)
            wot[rows, half * BLOCK : (half + 1) * BLOCK] = wo_ref[half, :, rows].T

    @pl.when(s < SECTIONS - 4)
    def _():
        pl.semaphore_wait(gate, 1)
        for i in range(PIECES):
            across(own_row, i).start()

    for i in range(PIECES):
        across(far_row, i).wait_recv()
        beside(far_row, i, PIECES + i).start()

    for i in range(PIECES):
        beside(near_row, i, i).wait_recv()
        beside(cross_row, i, PIECES + i).wait_recv()

    def ag_copy(k, dx):
        return remote(
            ag_buf.at[k], g_buf.at[k, x_pos], ag_send.at[k], ag_recv.at[k], s - 1, peer(dx, 0, 0)
        )

    def share_g(k):
        return remote(g_buf.at[k], g_in.at[k], g_send.at[k], g_recv.at[k], s, peer(0, 0, 1))

    def share_result(k):
        return remote(
            side_buf.at[k], side_in.at[k], side_send.at[k], side_recv.at[k], s, peer(0, 0, 1)
        )

    def first_half(k):
        first = pl.multiple_of(first_token(k), ROWS)

        @pl.when(s < SECTIONS - 1)
        def _():
            all_of(g_buf.at[k], ag_recv.at[k]).wait()

        g = jnp.concatenate([g_buf[k, i] for i in range(4)], axis=1)
        og = heads_to_rows(dot(g, wot[...]).astype(BF16))
        prob_grad = dot(og, v_t[...])
        probs = p_buf[k]
        delta = jnp.sum(probs * prob_grad, axis=-1, keepdims=True)
        score_grad = (probs * (prob_grad - delta)).astype(BF16)
        dq = (dot(score_grad, k_low[...]) * SCALE).astype(BF16)
        dkv_acc[:, :HEAD_DIM] += dot(score_grad, q_low[k], 0, 0) * SCALE
        dkv_acc[:, HEAD_DIM:] += dot(p_low_t[k], og)
        dkv = dkv_acc[pl.ds(first, ROWS), :].astype(BF16)
        keyval = jnp.concatenate(
            [k_low[pl.ds(first, ROWS), :], v_low[pl.ds(first, ROWS), :]], axis=1
        )
        stat = jnp.sum(rows_to_heads(dq.astype(F32) * q_hat[k]), axis=-1, keepdims=True)
        stat += jnp.sum(dkv.astype(F32) * keyval.astype(F32), axis=-1, keepdims=True)
        r = r_buf[c_pos, pl.ds(first, ROWS), :]
        stat = stat * (r * r / WIDTH)
        grads = jnp.concatenate([rows_to_heads(dq), dkv], axis=1)
        for j, dx in enumerate(HOPS):
            block = pl.ds(pl.multiple_of((x_pos + dx) % 4 * SLICE, SLICE), SLICE)
            part = dot(grads, wc[:, block]) * (r * gain_ref[:, block].astype(F32))
            part -= x_ref[c_pos, pl.ds(first, ROWS), block].astype(F32) * stat
            part_buf[k, j] = part.astype(BF16)
            for dz in (1, 0):
                if (dx, dz) == (0, 0):
                    continue
                remote(
                    part_buf.at[k, j], rs_buf.at[k, PEERS.index((dx, dz))],
                    rs_send.at[k], rs_recv.at[k], s, peer(dx, dz, 0),
                ).start()

    def second_half(k):
        first = pl.multiple_of(first_token(k), ROWS)
        total = g_buf[k, x_pos].astype(F32) + part_buf[k, len(HOPS) - 1].astype(F32)
        all_of(rs_buf.at[k], rs_recv.at[k]).wait()
        for j in range(len(PEERS)):
            total += rs_buf[k, j].astype(F32)
        ag_buf[k] = total.astype(BF16)

        @pl.when(s > 0)
        def _():
            for dx in HOPS:
                ag_copy(k, dx).start()

        half = jnp.where(z_pos == 0, total[:, : 2 * BLOCK], total[:, 2 * BLOCK :])
        left, right = half[:, :BLOCK], half[:, BLOCK:]
        side_buf[k] = jnp.where(c_pos == 0, right, left).astype(BF16)
        share_result(k).start()
        out_ref[c_pos, pl.ds(first, ROWS), :] = jnp.where(c_pos == 0, left, right).astype(BF16)

    def step(k, carry):
        @pl.when(k < CHUNKS)
        def _():
            first_half(k)

        @pl.when(k >= LAG)
        def _():
            second_half(k - LAG)

        return carry

    lax.fori_loop(0, CHUNKS + LAG, step, 0)

    for k in range(CHUNKS):
        share_g(k).start()
    share_att.wait_recv()
    att_out[c_pos] = att_own[...]
    att_out[other] = att_in[...]
    g_out[c_pos] = g_buf[...]
    for k in range(CHUNKS):
        share_g(k).wait_recv()
        g_out[other, k] = g_in[k]
    for k in range(CHUNKS):
        first = first_token(k)
        share_result(k).wait_recv()
        out_ref[other, first : first + ROWS, :] = side_in[k]

    for copy in (*kvt_copies, share_q, share_o, share_att):
        copy.wait_send()
    for i in range(PIECES):
        across(own_row, i).wait_send()
        beside(own_row, i, i).wait_send()
        beside(far_row, i, PIECES + i).wait_send()

    def drain(k, carry):
        all_of(rs_buf.at[k], rs_send.at[k]).wait()
        share_g(k).wait_send()
        share_result(k).wait_send()

        @pl.when(s > 0)
        def _():
            all_of(g_buf.at[k], ag_send.at[k]).wait()

        return carry

    lax.fori_loop(0, CHUNKS, drain, 0)

    @pl.when(s >= 4)
    def _():
        pl.semaphore_signal(gate, inc=1, device_id=(s - 4, d), device_id_type=MESH)


def relay(x, top, wq, wkv, wo, gain):
    vmem = pl.BlockSpec(memory_space=pltpu.VMEM)
    hbm = pl.BlockSpec(memory_space=pl.ANY)
    dma = pltpu.SemaphoreType.DMA
    return pl.pallas_call(
        kernel,
        out_shape=(
            jax.ShapeDtypeStruct((MICRO, TOKENS, BLOCK), BF16),
            jax.ShapeDtypeStruct((MICRO, CHUNKS, ROWS, BLOCK), BF16),
            jax.ShapeDtypeStruct((MICRO, CHUNKS, 4, ROWS, SLICE), BF16),
        ),
        in_specs=[hbm] * 5 + [vmem],
        out_specs=(vmem, vmem, vmem),
        scratch_shapes=[
            pltpu.VMEM((MICRO, TOKENS, WIDTH), BF16),
            pltpu.VMEM((MICRO, TOKENS, WIDTH), BF16),
            pltpu.VMEM((2, WIDTH, BLOCK), BF16),
            pltpu.VMEM((2, BLOCK, WIDTH), BF16),
            pltpu.VMEM((KV_ROW + BLOCK, WIDTH), BF16),
            pltpu.VMEM((WIDTH, KV_ROW), BF16),
            pltpu.VMEM((MICRO, TOKENS, WIDTH), BF16),
            pltpu.VMEM((MICRO, TOKENS, 1), F32),
            pltpu.VMEM((CHUNKS, HEADS * ROWS, HEAD_DIM), F32),
            pltpu.VMEM((CHUNKS, HEADS * ROWS, HEAD_DIM), BF16),
            pltpu.VMEM((BLOCK, MICRO * TOKENS), BF16),
            pltpu.VMEM((HEAD_DIM, TOKENS), BF16),
            pltpu.VMEM((HEAD_DIM, TOKENS), BF16),
            pltpu.VMEM((TOKENS, HEAD_DIM), BF16),
            pltpu.VMEM((TOKENS, HEAD_DIM), BF16),
            pltpu.VMEM((CHUNKS, HEADS * ROWS, TOKENS), F32),
            pltpu.VMEM((CHUNKS, TOKENS, HEADS * ROWS), BF16),
            pltpu.VMEM((TOKENS, BLOCK), F32),
            pltpu.VMEM((CHUNKS, 4, ROWS, SLICE), BF16),
            pltpu.VMEM((CHUNKS, 4, ROWS, SLICE), BF16),
            pltpu.VMEM((CHUNKS, ROWS, BLOCK), BF16),
            pltpu.VMEM((CHUNKS, ROWS, BLOCK), BF16),
            pltpu.VMEM((CHUNKS, ROWS, BLOCK), BF16),
            pltpu.VMEM((CHUNKS, len(HOPS), ROWS, SLICE), BF16),
            pltpu.VMEM((CHUNKS, len(PEERS), ROWS, SLICE), BF16),
            pltpu.VMEM((CHUNKS, ROWS, SLICE), BF16),
            pltpu.VMEM((CHUNKS, ROWS, BLOCK), BF16),
            pltpu.VMEM((CHUNKS, ROWS, BLOCK), BF16),
            dma((5,)),
            dma((CHUNKS,)),
            dma((CHUNKS,)),
            dma((CHUNKS,)),
            dma((CHUNKS,)),
            dma((2,)),
            dma((2,)),
            dma((CHUNKS,)),
            dma((CHUNKS,)),
            dma((CHUNKS,)),
            dma((CHUNKS,)),
            dma((2,)),
            dma((3,)),
            dma((3,)),
            dma((PIECES,)),
            dma((PIECES,)),
            dma((2 * PIECES,)),
            dma((2 * PIECES,)),
            pltpu.SemaphoreType.REGULAR,
        ],
        compiler_params=pltpu.CompilerParams(
            collective_id=0, has_side_effects=True, vmem_limit_bytes=60 * 1024 * 1024
        ),
        name="relay",
    )(x, top, wq, wkv, wo, gain)


def weight_kernel(block_ref, att_ref, g_ref, grad_ref):
    attended = att_ref[...].reshape(MICRO * TOKENS, BLOCK)
    g = g_ref[...].reshape(MICRO * TOKENS, SLICE)
    grad_ref[...] = dot(attended, g, 0, 0) * block_ref[0].astype(F32)


def weight_grad(new_block, att, g):
    return pl.pallas_call(
        weight_kernel,
        out_shape=jax.ShapeDtypeStruct((BLOCK, WIDTH), F32),
        grid=(4,),
        in_specs=[
            pl.BlockSpec(memory_space=pltpu.SMEM),
            pl.BlockSpec((MICRO, CHUNKS, ROWS, BLOCK), lambda i: (0, 0, 0, 0)),
            pl.BlockSpec((MICRO, CHUNKS, 1, ROWS, SLICE), lambda i: (0, 0, i, 0, 0)),
        ],
        out_specs=pl.BlockSpec((BLOCK, SLICE), lambda i: (0, i)),
        compiler_params=pltpu.CompilerParams(vmem_limit_bytes=60 * 1024 * 1024),
        name="weight_grad",
    )(new_block, att, g)


def body(layer_inputs, top_grad, w_query, w_keyval, w_out, norm_gain, new_block):
    stream, att, g = relay(
        layer_inputs[0], top_grad, w_query[0], w_keyval[0].T, w_out[0], norm_gain
    )
    return stream[None], weight_grad(new_block, att, g)[None]


def solution(mesh):
    in_specs = (
        P("section", None, None, None),
        P(),
        P("section", None, "dp"),
        P("section", None, "dp"),
        P("section", "dp", None),
        P("section", None),
        P("section"),
    )
    out_specs = (P("section", None, None, "dp"), P("section", "dp", None))
    return jax.shard_map(body, mesh=mesh, in_specs=in_specs, out_specs=out_specs, check_vma=False)
```
